512 devices in a mesh: attn: 32 (over z_lo, y), exp: 8 (over x, core), shard: 2 (over z_hi).
Axes of the slice: x: 4, y: 4, z: 16 (z_hi: 2, z_lo: 8; z = z_hi * 8 + z_lo), core: 2. Of those that a mesh axis runs over, the one named last changes fastest.
Arguments:
- tokens: bfloat16 [8192, 3584], P(('attn', 'shard'), 'exp'), may hold values from -6 to 6
- route_ids: int32 [8192, 1], P(('attn', 'shard')), may hold values from 0 to 31; in each aligned block of 128 rows (0 to 127, 128 to 255, ...) at most 8 rows name the same one
- gate_values: float32 [8192, 1], P(('attn', 'shard')), may hold values from 0.2 to 1
- slot_table: int32 [32], replicated, may hold values from 0 to 31, each once
- w_gate: bfloat16 [32, 3584, 1024], P('attn', 'shard', 'exp'), may hold values from -0.09375 to 0.09375
- w_up: bfloat16 [32, 3584, 1024], P('attn', 'shard', 'exp'), may hold values from -0.09375 to 0.09375
- w_down: bfloat16 [32, 1024, 3584], P('attn', 'exp', 'shard'), may hold values from -0.1875 to 0.1875
- cotangent: bfloat16 [8192, 3584], P(('attn', 'shard'), 'exp'), may hold values from -6 to 6
Outputs:
- mixed: bfloat16 [8192, 3584], P(('attn', 'shard'), 'exp')
- token_grads: bfloat16 [8192, 3584], P(('attn', 'shard'), 'exp')
- grad_gate: float32 [32, 3584, 1024], P('attn', 'shard', 'exp')
- grad_up: float32 [32, 3584, 1024], P('attn', 'shard', 'exp')
- grad_down: float32 [32, 1024, 3584], P('attn', 'exp', 'shard')
The draws below stay inside these ranges and needn't reach their ends.
Inputs may be any that keep to these rules, and one draw needn't show every extreme that they name: `route_ids`: among the 128 tokens of one source group no expert is named more than 8 times, a bound that some block reaches. `slot_table`: each slot holds exactly one expert.
All inputs are finite; a program needn't handle non-finite values.
Results may differ from the reference program's by a relative error of at most 0.018.
Values may be sent and summed in bfloat16 or wider, within the bound.
A program may use at most 64 MiB of HBM per device.

```python
import math
import jax
import jax.numpy as jnp
import numpy as np
from jax import lax

D = 3584
HID_DEV = 128
HID = 1024
TOK_DEV = 128
SLOTS = 32
CAP = 8
TOKENS = 8192
N_ATTN = 32
N_EXP = 8
N_SHARD = 2


def block_levels(rng, extent, split, least, largest):
    loudness = 1.0
    for position, parts in split:
        draws = jax.random.uniform(jax.random.fold_in(jax.random.fold_in(rng, 6), position), (parts,), jnp.float32, least / len(split), largest / len(split))
        loudness = loudness * jnp.repeat(jnp.exp(draws), extent[position] // parts).reshape((-1,) + (1,) * (len(extent) - 1 - position))
    return loudness


def deal_out(stream_key, own, number, rows, amount, top, bound, lean):
    sequence = jax.random.permutation(stream_key, amount)
    packed, common = load_shares(amount, rows * top, bound, lean, True), load_shares(amount, rows * top, bound, lean, False)
    places = jnp.arange(amount)

    def named(sizes, turn):
        used = int((sizes > 0).sum())
        fixed = max(1, used // 4)
        passed = fixed + (places - fixed + turn * (used - fixed)) % max(1, amount - fixed)
        return jnp.zeros((amount,), jnp.int32).at[sequence[jnp.where(places < fixed, places, passed)]].set(jnp.asarray(sizes, jnp.int32))

    sizes = jnp.where(number % 4 == 0, named(packed, number // 4), named(common, number - number // 4 - 1))
    mixed = jax.random.permutation(jax.random.fold_in(own, 3), amount)
    donor, taker = mixed[0:amount // 2 * 2:2], mixed[1:amount // 2 * 2:2]
    room = jnp.minimum(sizes[donor] - 1, bound - sizes[taker]) // 2
    room = jnp.where((donor == sequence[0]) | (taker == sequence[0]) | (sizes[taker] == 0), 0, jnp.maximum(room, 0))
    passed = jax.random.randint(jax.random.fold_in(own, 4), (amount // 2,), 0, 1 << 20) % (room + 1)
    sizes = sizes.at[donor].add(-passed).at[taker].add(passed)
    labels = jnp.searchsorted(jnp.cumsum(sizes), jnp.arange(rows * top), side="right").astype(jnp.int32)
    grid = labels.reshape(top, rows).T
    grid = grid[jax.random.permutation(jax.random.fold_in(own, 1), rows)]
    turn = jax.random.randint(jax.random.fold_in(own, 2), (rows, 1), 0, top)
    return jnp.take_along_axis(grid, (jnp.arange(top)[None, :] + turn) % top, axis=1)


def load_shares(count, total, most, slope, full):
    weights = [(1 << 20) // math.isqrt(rank ** slope) + 1 for rank in range(1, count + 1)]
    largest = most if full else min(most, max(-(-total // count), total * weights[0] // sum(weights)))
    least = 1 if total - largest >= count - 1 else 0
    counts, rest = [largest] + [least] * (count - 1), total - largest - least * (count - 1)
    while rest > 0:
        movable = [i for i in range(1, count) if counts[i] < largest] or [i for i in range(1, count) if counts[i] < most]
        pool, remaining = sum([weights[i] for i in movable]), rest
        for i in movable:
            extra = min(most - counts[i], max(1, remaining * weights[i] // pool), rest)
            counts[i] = counts[i] + extra
            rest = rest - extra
    return np.array(counts)


def noise(rng, extent, deviation, reach, pieces=(), held_as=jnp.bfloat16):
    result = jax.random.normal(rng, extent, jnp.float32) * deviation
    if len(pieces) > 0:
        result = block_levels(rng, extent, pieces, -0.22, 0.18) * result
    return jnp.clip(result, min=-reach, max=reach).astype(held_as)


def setup_inputs(seed: int = 0) -> dict:
    arg_keys = jax.random.split(jax.random.key(seed), 9)
    tokens = noise(arg_keys[0], (TOKENS, D), 1.0, 6.0, ((0, 64), (1, 8)))
    route_ids_keys = jax.random.split(jax.random.fold_in(arg_keys[1], 1), TOKENS // TOK_DEV)
    route_ids_turns = jax.random.permutation(jax.random.fold_in(arg_keys[1], 3), TOKENS // TOK_DEV)
    route_ids = jax.vmap(lambda own, number: deal_out(jax.random.fold_in(arg_keys[1], 2), own, number, TOK_DEV, SLOTS, 1, CAP, 2))(route_ids_keys, route_ids_turns).reshape((TOKENS, 1))
    gate_values = jnp.clip(0.2 + 0.8 * jax.random.uniform(arg_keys[2], (TOKENS, 1), jnp.float32) ** block_levels(arg_keys[2], (TOKENS, 1), ((0, 64),), -0.2, 0.2), 0.2, 1.0)
    slot_table = jax.random.permutation(arg_keys[3], SLOTS).astype(jnp.int32)
    w_gate = noise(arg_keys[4], (SLOTS, D, HID), D ** -0.5, 0.09375, ((0, 32), (1, 2), (2, 8)))
    w_up = noise(arg_keys[5], (SLOTS, D, HID), D ** -0.5, 0.09375, ((0, 32), (1, 2), (2, 8)))
    w_down = noise(arg_keys[6], (SLOTS, HID, D), HID ** -0.5, 0.1875, ((0, 32), (1, 8), (2, 2)))
    cotangent = noise(arg_keys[7], (TOKENS, D), 1.0, 6.0, ((0, 64), (1, 8)))
    return dict(tokens=tokens, route_ids=route_ids, gate_values=gate_values, slot_table=slot_table, w_gate=w_gate, w_up=w_up, w_down=w_down, cotangent=cotangent)


def slot_places(id_block, table):
    slot_count = table.shape[0]
    experts = jnp.arange(slot_count, dtype=jnp.int32)
    slot_of = jnp.sum(jnp.where(id_block == experts[None, :], table[None, :], 0), axis=1).astype(jnp.int32)
    member = (slot_of[:, None] == experts[None, :]).astype(jnp.int32)
    ranks = jnp.sum((jnp.cumsum(member, axis=0) - member) * member, axis=1).astype(jnp.int32)
    target = slot_of * CAP + ranks
    positions = jnp.arange(slot_count * CAP, dtype=jnp.int32)
    return (positions[:, None] == target[None, :]).astype(jnp.float32)


def rounded(values):
    narrow = lax.optimization_barrier(values.astype(jnp.bfloat16))
    return narrow.astype(jnp.float32)


def slot_work(inputs):
    x_slot, dy_slot, gate_w, up_w, down_w = inputs
    x_full = x_slot.astype(jnp.float32)
    dy_full = dy_slot.astype(jnp.float32)
    gate_f = gate_w.astype(jnp.float32)
    up_f = up_w.astype(jnp.float32)
    down_f = down_w.astype(jnp.float32)
    shard_count, row_count = x_full.shape[0], x_full.shape[1]
    pre_gate = jnp.einsum('srd,dh->srh', x_full, gate_f)
    pre_up = jnp.einsum('srd,dh->srh', x_full, up_f)
    hidden = rounded(jax.nn.silu(pre_gate) * pre_up)
    grouped = hidden.reshape(shard_count, row_count, N_EXP, HID_DEV)
    partial_value = jnp.einsum('srek,ekd->sred', grouped, down_f.reshape(N_EXP, HID_DEV, D))
    out_rows = jnp.sum(rounded(partial_value), axis=2).astype(jnp.bfloat16)
    d_hidden = jnp.einsum('srd,hd->srh', dy_full, down_f)
    grad_down = jnp.einsum('srh,srd->hd', hidden, dy_full)
    sigma = jax.nn.sigmoid(pre_gate)
    d_gate = rounded(d_hidden * pre_up * sigma * (1.0 + pre_gate * (1.0 - sigma)))
    d_up = rounded(d_hidden * pre_gate * sigma)
    grad_gate = jnp.einsum('srd,srh->dh', x_full, d_gate)
    grad_up = jnp.einsum('srd,srh->dh', x_full, d_up)
    in_part = jnp.einsum('srek,dek->sred', d_gate.reshape(shard_count, row_count, N_EXP, HID_DEV), gate_f.reshape(D, N_EXP, HID_DEV))
    in_part = in_part + jnp.einsum('srek,dek->sred', d_up.reshape(shard_count, row_count, N_EXP, HID_DEV), up_f.reshape(D, N_EXP, HID_DEV))
    in_rows = jnp.sum(rounded(in_part), axis=2).astype(jnp.bfloat16)
    return out_rows, in_rows, grad_gate, grad_up, grad_down


def reference(tokens, route_ids, gate_values, slot_table, w_gate, w_up, w_down, cotangent):
    groups = N_ATTN * N_SHARD
    places = jax.vmap(lambda block: slot_places(block, slot_table))(route_ids.reshape(groups, TOK_DEV, 1))
    gates = gate_values.reshape(groups, TOK_DEV, 1)
    x_src = tokens.reshape(groups, TOK_DEV, D).astype(jnp.float32)
    dy_src = (gates * cotangent.reshape(groups, TOK_DEV, D).astype(jnp.float32)).astype(jnp.bfloat16).astype(jnp.float32)
    x_rows = jnp.einsum('qrt,qtd->qrd', places, x_src).astype(jnp.bfloat16)
    dy_rows = jnp.einsum('qrt,qtd->qrd', places, dy_src).astype(jnp.bfloat16)

    def to_slots(array):
        shaped = array.reshape(N_ATTN, N_SHARD, SLOTS, CAP, D).transpose(2, 1, 0, 3, 4)
        return shaped.reshape(SLOTS, N_SHARD, N_ATTN * CAP, D)

    def to_sources(array):
        shaped = array.reshape(SLOTS, N_SHARD, N_ATTN, CAP, D).transpose(2, 1, 0, 3, 4)
        return shaped.reshape(groups, SLOTS * CAP, D)

    out_rows, in_rows, grad_gate, grad_up, grad_down = lax.map(slot_work, (to_slots(x_rows), to_slots(dy_rows), w_gate, w_up, w_down))
    combined = jnp.einsum('qrt,qrd->qtd', places, to_sources(out_rows).astype(jnp.float32))
    mixed = (gates * combined).astype(jnp.bfloat16).reshape(TOKENS, D)
    returned = jnp.einsum('qrt,qrd->qtd', places, to_sources(in_rows).astype(jnp.float32))
    token_grads = returned.astype(jnp.bfloat16).reshape(TOKENS, D)
    return mixed, token_grads, grad_gate, grad_up, grad_down
```

```python
import functools

import jax
import jax.numpy as jnp
from jax import lax
from jax.experimental import pallas as pl
from jax.experimental.pallas import tpu as pltpu
from jax.sharding import PartitionSpec as P

CHUNKS = 4
WIDE = 896
HALF = 448
WINDOW = 512
F32 = jnp.float32
BF16 = jnp.bfloat16


def base_offset(chunk, pair):
    first = jnp.where(chunk == 0, 0, chunk)
    second = jnp.where(chunk == 0, 4, 8 - chunk)
    return jnp.where(pair == 0, first, second)


def place():
    a, e, s = lax.axis_index("attn"), lax.axis_index("exp"), lax.axis_index("shard")
    return a % 4, a // 4 + 8 * s, e // 2, e % 2, s


def device(y, z, x, c):
    return {"attn": (z % 8) * 4 + y, "exp": 2 * x + c, "shard": z // 8}


def send(src, dst, send_sem, recv_sem, target):
    return pltpu.make_async_remote_copy(
        src_ref=src,
        dst_ref=dst,
        send_sem=send_sem,
        recv_sem=recv_sem,
        device_id=target,
        device_id_type=pl.DeviceIdType.MESH,
    )


def wait_for(ref, sem):
    pltpu.make_async_copy(ref, ref, sem).wait()


def last_last(a, b):
    return lax.dot_general(a, b, (((1,), (1,)), ((), ())), preferred_element_type=F32)


def first_first(a, b):
    return lax.dot_general(a, b, (((0,), (0,)), ((), ())), preferred_element_type=F32)


def dot(a, b):
    return jnp.dot(a, b, preferred_element_type=F32)


def kernel(
    xs, pp, wg, wu, wd, fin, gg, gu, gd,
    tok, sb, rows, wgu, acc, es, er, lg, os, orr, cs, xr, rb, rr, tb, tr,
    tok_s, tok_r, d_s, d_r, ag_s, ag_r, sf_s, sf_r, e_s, e_r, o_s, o_r, x_s, x_r, b_s, b_r, t_s, t_r,
):
    y, z, x, c, s = place()
    other = 3 - x
    p_own = jnp.where(x // 2 == s, 0, 1)
    qi_own = jnp.where(p_own == 0, x, other) - 2 * s
    h_src = jnp.where(c == 0, x, other) // 2
    h_fin = x // 2
    x_fin = jnp.where(p_own == 0, x, other)
    has_self = (c == 0) & (p_own == 0)
    sibling = device(y, z, x, 1 - c)
    partner = device(y, (z + 8) % 16, x, c)

    def piece_of(xx):
        p = jnp.where(xx // 2 == s, 0, 1)
        return jnp.where(p == 0, xx, 3 - xx) - 2 * s, p

    barrier = pltpu.get_barrier_semaphore()

    def greet(target):
        pl.semaphore_signal(barrier, inc=1, device_id=target, device_id_type=pl.DeviceIdType.MESH)

    greet(sibling)
    greet(partner)
    for r in (1, 2, 3):
        greet(device(y, z, (x + r) % 4, c))

    @pl.when(c == 0)
    def _():
        greet(device(y, z, x, 1))

    @pl.when(c == 1)
    def _():
        greet(device(y, z, other, 0))
        greet(device(y, z, other, 1))

    def greet_sources(i, carry):
        @pl.when(jnp.logical_not(has_self & (i == 0)))
        def _():
            greet(device((y + p_own + 2 * c) % 4, (z + i) % 16, x, p_own))

        return carry

    lax.fori_loop(0, 16, greet_sources, 0)
    x_back = jnp.where(c == 0, x, other)

    def greet_owners(i, carry):
        c_r = i % 2
        zz = 8 * h_fin + i // 2

        @pl.when(jnp.logical_not(has_self & (c_r == 0) & (zz == z)))
        def _():
            greet(device((y + 8 - c - 2 * c_r) % 4, zz, x_back, c_r))

        return carry

    lax.fori_loop(0, 16, greet_owners, 0)

    for q in range(2):
        wgu[q, :, 0:128] = wg[q * WIDE : (q + 1) * WIDE, :]
        wgu[q, :, 128:256] = wu[q * WIDE : (q + 1) * WIDE, :]

    pl.semaphore_wait(barrier, 5 + 1 + c + 32 - 2 * has_self.astype(jnp.int32))

    @pl.when(c == 0)
    def _():
        pltpu.make_async_copy(xs, tok.at[0], tok_r.at[0]).start()
        send(xs, tok.at[0], tok_s.at[0], tok_r.at[0], device(y, z, other, 1)).start()

    @pl.when(c == 1)
    def _():
        send(xs, tok.at[1], tok_s.at[0], tok_r.at[1], device(y, z, other, 1)).start()
        send(xs, tok.at[1], tok_s.at[1], tok_r.at[1], device(y, z, x, 0)).start()

    wait_for(tok.at[0], tok_r.at[0])
    wait_for(tok.at[1], tok_r.at[1])
    places = pp[...]
    left, right = tok[0], tok[1]
    whole = jnp.concatenate([left[:, :384], left[:, 384:] + right[:, :128], right[:, 128:]], axis=1)
    sb[...] = dot(places, whole).astype(BF16).reshape(16, 16, WIDE)

    def dispatch(i, carry):
        k, j, c_r = i // 4, (i // 2) % 2, i % 2
        zd = (z + 16 - base_offset(k, j)) % 16
        hi = jnp.where(zd // 8 == h_src, 0, 1)
        target = device((y + 8 - c - 2 * c_r) % 4, 8 * h_src + zd % 8, x, c_r)
        q_t = jnp.where(c == 0, x, other)
        there = rows.at[q_t - 2 * h_src, k, c_r, c, 2 * j + hi]
        mine = has_self & (i == 0)

        @pl.when(mine)
        def _():
            pltpu.make_async_copy(sb.at[i], there, d_r.at[k]).start()

        @pl.when(jnp.logical_not(mine))
        def _():
            send(sb.at[i], there, d_s.at[jnp.where(i == 0, CHUNKS, k)], d_r.at[k], target).start()

        return carry

    lax.fori_loop(0, 16, dispatch, 0)

    def gather(k):
        own = rows.at[qi_own, k, c, p_own]
        wait_for(own, d_r.at[k])
        for r in (1, 2, 3):
            send(own, own, ag_s.at[k, r - 1], ag_r.at[k, r - 1], device(y, z, (x + r) % 4, c)).start()

    def forward(k):
        for r in (1, 2, 3):
            qi, p = piece_of((x + 4 - r) % 4)
            wait_for(rows.at[qi, k, c, p], ag_r.at[k, r - 1])
        for q in range(2):
            send(rows.at[q, k, c], rows.at[q, k, c], sf_s.at[k, q], sf_r.at[k, q], sibling).start()

    def project(k):
        for q in range(2):
            wait_for(rows.at[q, k, 1 - c], sf_r.at[k, q])
        both = jnp.zeros((256, 256), F32)
        down = jnp.zeros((256, 128), F32)
        for q in range(2):
            block = rows[q, k].reshape(256, WIDE)
            both = both + dot(block, wgu[q])
            down = down + last_last(block, wd[:, q * WIDE : (q + 1) * WIDE])
        part = jnp.concatenate(
            [both.reshape(16, 2, 8, 256)[:, 0], down.reshape(16, 2, 8, 128)[:, 1]], axis=-1
        )
        acc[k] = part.reshape(128, 384)
        pairs = part.reshape(8, 2, 8, 384)
        es[k] = jnp.concatenate([pairs[:, 1:], pairs[:, :1]], axis=1).reshape(128, 384).astype(BF16)
        send(es.at[k], er.at[k], e_s.at[k], e_r.at[k], partner).start()

    def expand(k):
        wait_for(er.at[k], e_r.at[k])
        total = acc[k] + er[k].astype(F32)
        gate, up, d_hid = total[:, :128], total[:, 128:256], total[:, 256:]
        sigma = jax.nn.sigmoid(gate)
        hidden = gate * sigma * up
        d_gate = d_hid * up * sigma * (1.0 + gate * (1.0 - sigma))
        d_up = d_hid * gate * sigma
        d_both = jnp.concatenate([d_gate, d_up], axis=1)
        nothing = jnp.zeros((16, 8, 128), F32)
        top = jnp.concatenate([d_both.reshape(16, 8, 256), nothing], axis=-1)
        low = jnp.concatenate([nothing, nothing, hidden.reshape(16, 8, 128)], axis=-1)
        lg[k] = jnp.stack([top, low], axis=1).reshape(256, 384).astype(BF16)
        hidden, d_both = hidden.astype(BF16), d_both.astype(BF16)
        for q in range(2):
            outs = dot(hidden, wd[:, q * WIDE : (q + 1) * WIDE]).reshape(16, 8, WIDE)
            ins = last_last(d_both, wgu[q]).reshape(16, 8, WIDE)
            mixed = jnp.stack([outs, ins], axis=1).reshape(2, 2, 4, 16, WIDE).astype(BF16)
            os[k, 0, q] = mixed[0]
            os[k, 1, q] = mixed[1]
        send(os.at[k, 1 - c], orr.at[k], o_s.at[k], o_r.at[k], sibling).start()

    def scatter(k):
        wait_for(orr.at[k], o_r.at[k])
        for q in range(2):
            cs[k, q] = (os[k, c, q].astype(F32) + orr[k, q].astype(F32)).astype(BF16)
        for r in (1, 2, 3):
            xx = (x + r) % 4
            qi, p = piece_of(xx)
            send(cs.at[k, qi, p], xr.at[k, r - 1], x_s.at[k, r - 1], x_r.at[k, r - 1], device(y, z, xx, c)).start()

    def give_back(k):
        for r in (1, 2, 3):
            wait_for(xr.at[k, r - 1], x_r.at[k, r - 1])
        total = cs[k, qi_own, p_own].astype(F32)
        for r in range(3):
            total = total + xr[k, r].astype(F32)
        rb[k] = total.astype(BF16)
        for j in range(2):
            for hi in range(2):
                zs = (z + base_offset(k, j) + 8 * hi) % 16
                target = device((y + p_own + 2 * c) % 4, zs, x_fin, p_own)
                there = rr.at[4 * k + 2 * j + c]
                first = (j == 0) and (hi == 0)
                mine = has_self & (k == 0) if first else None
                sem = b_s.at[k, 2 * j + hi]
                if first:

                    @pl.when(mine)
                    def _():
                        pltpu.make_async_copy(rb.at[k, 0], there, b_r.at[k]).start()

                    @pl.when(jnp.logical_not(mine))
                    def _():
                        send(rb.at[k, 0], there, sem, b_r.at[k], target).start()

                else:
                    send(rb.at[k, 2 * j + hi], there, sem, b_r.at[k], target).start()

    stages = ((gather, 0), (forward, 1), (project, 2), (expand, 6), (scatter, 7), (give_back, 8))

    def step(t, carry):
        for stage, lag in stages:

            @pl.when((t >= lag) & (t < lag + CHUNKS))
            def _():
                stage(t - lag)

        return carry

    lax.fori_loop(0, CHUNKS + 8, step, 0)

    factors = lg[...].reshape(1024, 384).T
    for q in range(2):

        def columns(n, carry):
            lanes = pl.ds(pl.multiple_of(n * 128, 128), 128)
            block = rows[q, :, :, :, :, :, lanes].reshape(1024, 128)
            grads = dot(factors, block)
            at = pl.ds(pl.multiple_of(q * WIDE + n * 128, 128), 128)
            gg[at, :] = grads[:128].T
            gu[at, :] = grads[128:256].T
            gd[:, at] = grads[256:]
            return carry

        lax.fori_loop(0, 7, columns, 0)

    for k in range(CHUNKS):
        wait_for(rr.at[pl.ds(4 * k, 4)], b_r.at[k])
    tb[...] = first_first(places, rr[...].reshape(256, WIDE)).astype(BF16)
    theirs = pl.ds(pl.multiple_of(384 * (1 - c), 128), WINDOW)
    ours = pl.ds(pl.multiple_of(384 * c, 128), WINDOW)
    swap = send(tb.at[:, theirs], tr, t_s, t_r, sibling)
    swap.start()

    wait_for(xs, tok_s.at[0])

    @pl.when(c == 1)
    def _():
        wait_for(xs, tok_s.at[1])

    wait_for(sb.at[pl.ds(1, 3)], d_s.at[0])
    for k in range(1, CHUNKS):
        wait_for(sb.at[pl.ds(4 * k, 4)], d_s.at[k])

    @pl.when(jnp.logical_not(has_self))
    def _():
        wait_for(sb.at[0], d_s.at[CHUNKS])
        wait_for(rb.at[0, 0], b_s.at[0, 0])

    def drain(k, carry):
        for r in range(3):
            wait_for(xr.at[k, r], ag_s.at[k, r])
            wait_for(xr.at[k, r], x_s.at[k, r])
        for q in range(2):
            wait_for(rows.at[q, k, c], sf_s.at[k, q])
        wait_for(es.at[k], e_s.at[k])
        wait_for(orr.at[k], o_s.at[k])
        for i in range(4):
            if i == 0:

                @pl.when(k > 0)
                def _():
                    wait_for(rb.at[k, 0], b_s.at[k, 0])

            else:
                wait_for(rb.at[k, i], b_s.at[k, i])
        return carry

    lax.fori_loop(0, CHUNKS, drain, 0)
    swap.wait()
    fin[...] = tb[:, ours] + tr[...]


def shards(tokens, route_ids, gate_values, slot_table, w_gate, w_up, w_down, cotangent):
    y, z, x, c, _ = place()
    experts = jnp.arange(32, dtype=jnp.int32)
    slot_of = jnp.sum(jnp.where(route_ids == experts[None, :], slot_table[None, :], 0), axis=1)
    member = (slot_of[:, None] == experts[None, :]).astype(jnp.int32)
    ranks = jnp.sum((jnp.cumsum(member, axis=0) - member) * member, axis=1)

    index = jnp.arange(256, dtype=jnp.int32)
    block, kind, rank = index // 16, (index // 8) % 2, index % 8
    chunk, pair, core = block // 4, (block // 2) % 2, block % 2
    slot = ((z + 16 - base_offset(chunk, pair)) % 8) * 4 + (y + 8 - c - 2 * core) % 4
    hit = (slot[:, None] == slot_of[None, :]) & (rank[:, None] == ranks[None, :])
    hit = jnp.stack([hit & (kind == 0)[:, None], hit & (kind == 1)[:, None]], axis=1)
    places = hit.reshape(256, 256).astype(BF16)

    weighted = (gate_values * cotangent.astype(F32)).astype(BF16)
    stacked = jnp.concatenate([tokens, weighted], axis=0)
    stacked = jnp.where(
        c == 0, jnp.pad(stacked, ((0, 0), (0, 64))), jnp.pad(stacked, ((0, 0), (64, 0)))
    )
    vmem = pl.BlockSpec(memory_space=pltpu.VMEM)
    sem = pltpu.SemaphoreType.DMA
    fin, grad_gate, grad_up, grad_down = pl.pallas_call(
        kernel,
        name="expert_layer",
        out_shape=(
            jax.ShapeDtypeStruct((256, WINDOW), BF16),
            jax.ShapeDtypeStruct((1792, 128), F32),
            jax.ShapeDtypeStruct((1792, 128), F32),
            jax.ShapeDtypeStruct((128, 1792), F32),
        ),
        in_specs=[vmem] * 5,
        out_specs=(vmem,) * 4,
        scratch_shapes=[
            pltpu.VMEM((2, 256, WINDOW), BF16),
            pltpu.VMEM((16, 16, WIDE), BF16),
            pltpu.VMEM((2, CHUNKS, 2, 2, 4, 16, WIDE), BF16),
            pltpu.VMEM((2, WIDE, 256), BF16),
            pltpu.VMEM((CHUNKS, 128, 384), F32),
            pltpu.VMEM((CHUNKS, 128, 384), BF16),
            pltpu.VMEM((CHUNKS, 128, 384), BF16),
            pltpu.VMEM((CHUNKS, 256, 384), BF16),
            pltpu.VMEM((CHUNKS, 2, 2, 2, 4, 16, WIDE), BF16),
            pltpu.VMEM((CHUNKS, 2, 2, 4, 16, WIDE), BF16),
            pltpu.VMEM((CHUNKS, 2, 2, 4, 16, WIDE), BF16),
            pltpu.VMEM((CHUNKS, 3, 4, 16, WIDE), BF16),
            pltpu.VMEM((CHUNKS, 4, 16, WIDE), BF16),
            pltpu.VMEM((16, 16, WIDE), BF16),
            pltpu.VMEM((256, WIDE), BF16),
            pltpu.VMEM((256, WINDOW), BF16),
            sem((2,)),
            sem((2,)),
            sem((CHUNKS + 1,)),
            sem((CHUNKS,)),
            sem((CHUNKS, 3)),
            sem((CHUNKS, 3)),
            sem((CHUNKS, 2)),
            sem((CHUNKS, 2)),
            sem((CHUNKS,)),
            sem((CHUNKS,)),
            sem((CHUNKS,)),
            sem((CHUNKS,)),
            sem((CHUNKS, 3)),
            sem((CHUNKS, 3)),
            sem((CHUNKS, 4)),
            sem((CHUNKS,)),
            sem,
            sem,
        ],
        compiler_params=pltpu.CompilerParams(
            collective_id=0, has_side_effects=True, vmem_limit_bytes=48 * 2**20
        ),
    )(stacked, places, w_gate[0], w_up[0], w_down[0])
    fin = jnp.where(c == 0, fin[:, :HALF], fin[:, 64:])
    mixed = (gate_values * fin[:128].astype(F32)).astype(BF16)
    return mixed, fin[128:], grad_gate[None], grad_up[None], grad_down[None]


def solution(mesh):
    in_specs = (
        P(("attn", "shard"), "exp"),
        P(("attn", "shard"), None),
        P(("attn", "shard"), None),
        P(),
        P("attn", "shard", "exp"),
        P("attn", "shard", "exp"),
        P("attn", "exp", "shard"),
        P(("attn", "shard"), "exp"),
    )
    out_specs = (
        P(("attn", "shard"), "exp"),
        P(("attn", "shard"), "exp"),
        P("attn", "shard", "exp"),
        P("attn", "shard", "exp"),
        P("attn", "exp", "shard"),
    )
    return jax.shard_map(shards, mesh=mesh, in_specs=in_specs, out_specs=out_specs, check_vma=False)
```

```python
import jax
import jax.numpy as jnp
from jax import lax
from jax.experimental import pallas as pl
from jax.experimental.pallas import tpu as pltpu
from jax.sharding import PartitionSpec as P

CHUNKS = 8
LAGS = (0, 3, 4, 5, 6, 8, 11, 12, 13, 14)
WIDE = 896
HALF = 448
KERNEL_VMEM = 60 * 2**20
F32 = jnp.float32
BF16 = jnp.bfloat16


def base_offset(chunk):
    half = chunk // 2
    odd = jnp.where(chunk == 1, 4, 8 - half)
    return jnp.where(chunk % 2 == 0, half, odd)


def place():
    a, e, s = lax.axis_index("attn"), lax.axis_index("exp"), lax.axis_index("shard")
    return a % 4, a // 4 + 8 * s, e // 2, e % 2, s


def device(y, z, x, c):
    return {"attn": (z % 8) * 4 + y, "exp": 2 * x + c, "shard": z // 8}


def send(src, dst, send_sem, recv_sem, target):
    return pltpu.make_async_remote_copy(
        src_ref=src,
        dst_ref=dst,
        send_sem=send_sem,
        recv_sem=recv_sem,
        device_id=target,
        device_id_type=pl.DeviceIdType.MESH,
    )


def wait_for(ref, sem):
    pltpu.make_async_copy(ref, ref, sem).wait()


def last_last(a, b):
    return lax.dot_general(a, b, (((1,), (1,)), ((), ())), preferred_element_type=F32)


def first_first(a, b):
    return lax.dot_general(a, b, (((0,), (0,)), ((), ())), preferred_element_type=F32)


def dot(a, b):
    return jnp.dot(a, b, preferred_element_type=F32)


def kernel(
    tokens_far, cot_far, ids_far, gates_far, table_far, wg, wu, wd_far,
    mixed_far, back_far, gg_far, gu_far, gd_far, mixed, back, gg, gu, gd, g_s, tokens, cotangent, ids, gates, table, tok, ex, pp, sb, rows, wgu, wd, acc, es, em, er, lg, os, orr, cs, fr, xr, rb, rr, tb, tr,
    i_r, w_r, tok_s, tok_r, d_s, d_r, ag_s, ag_r, sf_s, sf_r, e_s, e_r, o_s, o_r, x_s, x_r, b_s, b_r, t_s, t_r,
):
    y, z, x, c, s = place()
    other = 3 - x
    p_own = jnp.where(x // 2 == s, 0, 1)
    qi_own = jnp.where(p_own == 0, x, other) - 2 * s
    h_src = jnp.where(c == 0, x, other) // 2
    h_fin = x // 2
    x_fin = jnp.where(p_own == 0, x, other)
    has_self = (c == 0) & (p_own == 0)
    sibling = device(y, z, x, 1 - c)
    z_up, z_dn = device(y, (z + 4) % 16, x, c), device(y, (z + 12) % 16, x, c)

    def piece_of(xx):
        p = jnp.where(xx // 2 == s, 0, 1)
        return jnp.where(p == 0, xx, 3 - xx) - 2 * s, p

    loads = []
    for i, (far, near) in enumerate(
        ((tokens_far, tokens), (cot_far, cotangent), (ids_far, ids), (gates_far, gates), (table_far, table))
    ):
        loads.append(pltpu.make_async_copy(far, near, i_r.at[i]))
        loads[-1].start()

    barrier = pltpu.get_barrier_semaphore()

    def greet(target):
        pl.semaphore_signal(barrier, inc=1, device_id=target, device_id_type=pl.DeviceIdType.MESH)

    greet(sibling)
    greet(z_up)
    greet(z_dn)
    for r in (1, 3):
        greet(device(y, z, (x + r) % 4, c))

    @pl.when(c == 0)
    def _():
        greet(device(y, z, x, 1))

    @pl.when(c == 1)
    def _():
        greet(device(y, z, other, 0))
        greet(device(y, z, other, 1))

    def greet_sources(i, carry):
        @pl.when(jnp.logical_not(has_self & (i == 0)))
        def _():
            greet(device((y + p_own + 2 * c) % 4, (z + i) % 16, x, p_own))

        return carry

    lax.fori_loop(0, 16, greet_sources, 0)
    x_back = jnp.where(c == 0, x, other)

    def greet_owners(i, carry):
        c_r = i % 2
        zz = 8 * h_fin + i // 2

        @pl.when(jnp.logical_not(has_self & (c_r == 0) & (zz == z)))
        def _():
            greet(device((y + 8 - c - 2 * c_r) % 4, zz, x_back, c_r))

        return carry

    lax.fori_loop(0, 16, greet_owners, 0)

    weights = [pltpu.make_async_copy(wd_far.at[0], wd, w_r.at[0])]
    for q in range(2):
        half = pl.ds(q * WIDE, WIDE)
        weights.append(pltpu.make_async_copy(wg.at[0, half], wgu.at[q, :, pl.ds(0, 128)], w_r.at[1 + q]))
        weights.append(pltpu.make_async_copy(wu.at[0, half], wgu.at[q, :, pl.ds(128, 128)], w_r.at[3 + q]))
    for load in weights:
        load.start()
    for load in loads:
        load.wait()

    tok[:, 0:128] = tokens[...]
    tok[:, 128:256] = (gates[...] * cotangent[...].astype(F32)).astype(BF16)

    pl.semaphore_wait(barrier, 6 + c + 32 - 2 * has_self.astype(jnp.int32))

    across = device(y, z, other, 1)

    @pl.when(c == 0)
    def _():
        send(tok, ex.at[0], tok_s.at[0], tok_r.at[0], across).start()

    @pl.when(c == 1)
    def _():
        send(tok, ex.at[1], tok_s.at[1], tok_r.at[1], device(y, z, x, 0)).start()
        send(tok, ex.at[1], tok_s.at[0], tok_r.at[1], across).start()

    row32 = lax.broadcasted_iota(jnp.int32, (32, 128), 0)
    named = (jnp.broadcast_to(ids[...], (32, 128)) == row32).astype(BF16)
    renamed = jnp.broadcast_to(table[...], (32, 32)) == lax.broadcasted_iota(jnp.int32, (32, 32), 0)
    member = dot(renamed.astype(BF16), named)
    earlier = lax.broadcasted_iota(jnp.int32, (128, 128), 0) < lax.broadcasted_iota(
        jnp.int32, (128, 128), 1
    )
    before = dot(member.astype(BF16), earlier.astype(BF16))
    rank_of = jnp.sum(member * before, axis=0, keepdims=True).astype(jnp.int32)
    slot_of = jnp.sum(member * row32.astype(F32), axis=0, keepdims=True).astype(jnp.int32)
    index = lax.broadcasted_iota(jnp.int32, (256, 128), 0)
    block, kind, rank = index // 16, (index // 8) % 2, index % 8
    offset = base_offset(block // 2)
    slot = ((z + 16 - offset) % 8) * 4 + (y + 8 - c - 2 * (block % 2)) % 4
    hit = (slot == slot_of) & (rank == rank_of)
    pp[:, 0:128] = (hit & (kind == 0)).astype(BF16)
    pp[:, 128:256] = (hit & (kind == 1)).astype(BF16)

    @pl.when(c == 0)
    def _():
        ex[0] = tok[...]

    @pl.when(c == 1)
    def _():
        wait_for(ex.at[0], tok_r.at[0])

    wait_for(ex.at[1], tok_r.at[1])
    sb[...] = last_last(pp[...], ex[...].reshape(WIDE, 256)).astype(BF16).reshape(16, 16, WIDE)

    def dispatch(i, carry):
        k, c_r = i // 2, i % 2
        zd = (z + 16 - base_offset(k)) % 16
        hi = jnp.where(zd // 8 == h_src, 0, 1)
        target = device((y + 8 - c - 2 * c_r) % 4, 8 * h_src + zd % 8, x, c_r)
        q_t = jnp.where(c == 0, x, other)
        there = rows.at[q_t - 2 * h_src, k, c_r, c, hi]
        mine = has_self & (i == 0)

        @pl.when(mine)
        def _():
            pltpu.make_async_copy(sb.at[i], there, d_r.at[k]).start()

        @pl.when(jnp.logical_not(mine))
        def _():
            send(sb.at[i], there, d_s.at[jnp.where(i == 0, CHUNKS, k)], d_r.at[k], target).start()

        return carry

    def give_out(k):
        lax.fori_loop(2 * k, 2 * k + 2, dispatch, 0)

    up, down_x = device(y, z, (x + 1) % 4, c), device(y, z, (x + 3) % 4, c)
    qi_up, p_up = piece_of((x + 1) % 4)
    qi_dn, p_dn = piece_of((x + 3) % 4)
    qi_far, p_far = piece_of((x + 2) % 4)
    low, high = pl.ds(0, 1), pl.ds(1, 1)
    first, second = pl.ds(0, 32), pl.ds(32, 32)

    def gather(k):
        own = rows.at[qi_own, k, c, p_own]
        wait_for(own, d_r.at[k])
        send(own, own, ag_s.at[k, 0], ag_r.at[k, 0], up).start()
        send(own, own, ag_s.at[k, 1], ag_r.at[k, 1], down_x).start()

    def relay(k):
        wait_for(rows.at[qi_dn, k, c, p_dn], ag_r.at[k, 0])
        part = rows.at[qi_dn, k, c, p_dn, low]
        send(part, part, ag_s.at[k, 2], ag_r.at[k, 2], up).start()
        wait_for(rows.at[qi_up, k, c, p_up], ag_r.at[k, 1])
        part = rows.at[qi_up, k, c, p_up, high]
        send(part, part, ag_s.at[k, 3], ag_r.at[k, 3], down_x).start()

    def forward(k):
        wait_for(rows.at[qi_far, k, c, p_far, low], ag_r.at[k, 2])
        wait_for(rows.at[qi_far, k, c, p_far, high], ag_r.at[k, 3])
        for q in range(2):
            send(rows.at[q, k, c], rows.at[q, k, c], sf_s.at[k, q], sf_r.at[k, q], sibling).start()

    def project(k):
        for q in range(2):
            wait_for(rows.at[q, k, 1 - c], sf_r.at[k, q])
        both = jnp.zeros((128, 256), F32)
        down = jnp.zeros((128, 128), F32)
        for q in range(2):
            block = rows[q, k].reshape(128, WIDE)
            both = both + dot(block, wgu[q])
            down = down + last_last(block, wd[:, q * WIDE : (q + 1) * WIDE])
        part = jnp.concatenate(
            [both.reshape(8, 2, 8, 256)[:, 0], down.reshape(8, 2, 8, 128)[:, 1]], axis=-1
        )
        acc[k] = part.reshape(64, 384)
        pairs = part.reshape(4, 2, 8, 384)
        es[k] = jnp.concatenate([pairs[:, 1:], pairs[:, :1]], axis=1).reshape(64, 384).astype(BF16)
        send(es.at[k, first], em.at[k, first], e_s.at[k, 0], e_r.at[k, 0], z_up).start()
        send(es.at[k, second], em.at[k, second], e_s.at[k, 1], e_r.at[k, 1], z_dn).start()

    def hop(k):
        wait_for(em.at[k, first], e_r.at[k, 0])
        send(em.at[k, first], er.at[k, first], e_s.at[k, 2], e_r.at[k, 2], z_up).start()
        wait_for(em.at[k, second], e_r.at[k, 1])
        send(em.at[k, second], er.at[k, second], e_s.at[k, 3], e_r.at[k, 3], z_dn).start()

    def expand(k):
        wait_for(er.at[k, first], e_r.at[k, 2])
        wait_for(er.at[k, second], e_r.at[k, 3])
        total = acc[k] + er[k].astype(F32)
        gate, up, d_hid = total[:, :128], total[:, 128:256], total[:, 256:]
        sigma = jax.nn.sigmoid(gate)
        hidden = gate * sigma * up
        d_gate = d_hid * up * sigma * (1.0 + gate * (1.0 - sigma))
        d_up = d_hid * gate * sigma
        d_both = jnp.concatenate([d_gate, d_up], axis=1)
        nothing = jnp.zeros((8, 8, 128), F32)
        over = jnp.concatenate([d_both.reshape(8, 8, 256), nothing], axis=-1)
        under = jnp.concatenate([nothing, nothing, hidden.reshape(8, 8, 128)], axis=-1)
        lg[k] = jnp.stack([over, under], axis=1).reshape(128, 384).astype(BF16)
        hidden, d_both = hidden.astype(BF16), d_both.astype(BF16)
        for q in range(2):
            outs = dot(hidden, wd[:, q * WIDE : (q + 1) * WIDE]).reshape(8, 8, WIDE)
            ins = last_last(d_both, wgu[q]).reshape(8, 8, WIDE)
            shares = jnp.stack([outs, ins], axis=1).reshape(2, 2, 2, 16, WIDE).astype(BF16)
            os[k, 0, q] = shares[0]
            os[k, 1, q] = shares[1]
        send(os.at[k, 1 - c], orr.at[k], o_s.at[k], o_r.at[k], sibling).start()

    def scatter(k):
        wait_for(orr.at[k], o_r.at[k])
        for q in range(2):
            cs[k, q] = (os[k, c, q].astype(F32) + orr[k, q].astype(F32)).astype(BF16)
        send(cs.at[k, qi_far, p_far, low], fr.at[k, 0], x_s.at[k, 0], x_r.at[k, 0], up).start()
        send(cs.at[k, qi_far, p_far, high], fr.at[k, 1], x_s.at[k, 1], x_r.at[k, 1], down_x).start()

    def combine(k):
        wait_for(fr.at[k, 0], x_r.at[k, 0])
        cs[k, qi_up, p_up, 0:1] = (cs[k, qi_up, p_up, 0:1].astype(F32) + fr[k, 0].astype(F32)).astype(BF16)
        send(cs.at[k, qi_up, p_up], xr.at[k, 0], x_s.at[k, 2], x_r.at[k, 2], up).start()
        wait_for(fr.at[k, 1], x_r.at[k, 1])
        cs[k, qi_dn, p_dn, 1:2] = (cs[k, qi_dn, p_dn, 1:2].astype(F32) + fr[k, 1].astype(F32)).astype(BF16)
        send(cs.at[k, qi_dn, p_dn], xr.at[k, 1], x_s.at[k, 3], x_r.at[k, 3], down_x).start()

    def give_back(k):
        total = cs[k, qi_own, p_own].astype(F32)
        for r in range(2):
            wait_for(xr.at[k, r], x_r.at[k, 2 + r])
            total = total + xr[k, r].astype(F32)
        rb[k] = total.astype(BF16)
        there = rr.at[2 * k + c]
        for hi in range(2):
            zs = (z + base_offset(k) + 8 * hi) % 16
            target = device((y + p_own + 2 * c) % 4, zs, x_fin, p_own)
            go = send(rb.at[k, hi], there, b_s.at[k, hi], b_r.at[k], target)
            if hi == 0:
                mine = has_self & (k == 0)

                @pl.when(mine)
                def _():
                    pltpu.make_async_copy(rb.at[k, 0], there, b_r.at[k]).start()

                @pl.when(jnp.logical_not(mine))
                def _():
                    go.start()

            else:
                go.start()

    order = (give_out, gather, relay, forward, project, hop, expand, scatter, combine, give_back)
    stages = tuple(zip(order, LAGS))

    def step(t, carry):
        for stage, lag in stages:

            @pl.when((t >= lag) & (t < lag + CHUNKS))
            def _():
                stage(t - lag)

        return carry

    for load in weights:
        load.wait()
    lax.fori_loop(0, CHUNKS + LAGS[-1], step, 0)

    factors = lg[...].reshape(1024, 384).T
    for q in range(2):

        def columns(n, carry):
            lanes = pl.ds(pl.multiple_of(n * 128, 128), 128)
            block = rows[q, :, :, :, :, :, lanes].reshape(1024, 128)
            grads = dot(factors, block)
            at = pl.ds(pl.multiple_of(q * WIDE + n * 128, 128), 128)
            gg[at, :] = grads[:128].T
            gu[at, :] = grads[128:256].T
            gd[:, at] = grads[256:]
            return carry

        lax.fori_loop(0, 7, columns, 0)

    stores = [
        pltpu.make_async_copy(near, far, g_s.at[i])
        for i, (near, far) in enumerate(
            ((mixed, mixed_far), (back, back_far), (gg, gg_far), (gu, gu_far), (gd, gd_far))
        )
    ]
    for copy in stores[2:]:
        copy.start()
    for k in range(CHUNKS):
        wait_for(rr.at[pl.ds(2 * k, 2)], b_r.at[k])
    tb[...] = first_first(rr[...].reshape(256, WIDE), pp[...]).astype(BF16).reshape(2, HALF, 256)
    swap = send(tb.at[1 - c], tr, t_s, t_r, sibling)
    swap.start()

    wait_for(tok, tok_s.at[0])

    @pl.when(c == 1)
    def _():
        wait_for(tok, tok_s.at[1])

    wait_for(sb.at[1], d_s.at[0])
    for k in range(1, CHUNKS):
        wait_for(sb.at[pl.ds(2 * k, 2)], d_s.at[k])

    @pl.when(jnp.logical_not(has_self))
    def _():
        wait_for(sb.at[0], d_s.at[CHUNKS])
        wait_for(rb.at[0, 0], b_s.at[0, 0])

    def drain(k, carry):
        for r in range(2):
            wait_for(xr.at[k, r], ag_s.at[k, r])
            wait_for(fr.at[k, r], ag_s.at[k, 2 + r])
            wait_for(fr.at[k, r], x_s.at[k, r])
            wait_for(xr.at[k, r], x_s.at[k, 2 + r])
        for q in range(2):
            wait_for(rows.at[q, k, c], sf_s.at[k, q])
        wait_for(es.at[k, first], e_s.at[k, 0])
        wait_for(es.at[k, second], e_s.at[k, 1])
        wait_for(em.at[k, first], e_s.at[k, 2])
        wait_for(em.at[k, second], e_s.at[k, 3])
        wait_for(orr.at[k], o_s.at[k])
        for i in range(2):
            if i == 0:

                @pl.when(k > 0)
                def _():
                    wait_for(rb.at[k, 0], b_s.at[k, 0])

            else:
                wait_for(rb.at[k, i], b_s.at[k, i])
        return carry

    lax.fori_loop(0, CHUNKS, drain, 0)
    swap.wait()
    mixed[...] = (gates[...] * (tb[c, :, 0:128] + tr[:, 0:128]).astype(F32)).astype(BF16)
    stores[0].start()
    back[...] = tb[c, :, 128:256] + tr[:, 128:256]
    stores[1].start()
    for copy in stores:
        copy.wait()


def store(*refs):
    far, out, near, sems = refs[0:5], refs[5:10], refs[10:15], refs[15]
    order = (2, 3, 4, 0, 1)
    for i in order:
        pltpu.make_async_copy(far[i], near[i], sems.at[0, i]).start()
    for i in order:
        pltpu.make_async_copy(far[i], near[i], sems.at[0, i]).wait()
        pltpu.make_async_copy(near[i], out[i], sems.at[1, i]).start()
    for i in order:
        pltpu.make_async_copy(near[i], out[i], sems.at[1, i]).wait()


def shards(tokens, route_ids, gate_values, slot_table, w_gate, w_up, w_down, cotangent):
    hbm = pl.BlockSpec(memory_space=pltpu.HBM)
    sem = pltpu.SemaphoreType.DMA
    shapes = (
        jax.ShapeDtypeStruct((HALF, 128), BF16),
        jax.ShapeDtypeStruct((HALF, 128), BF16),
        jax.ShapeDtypeStruct((1792, 128), F32),
        jax.ShapeDtypeStruct((1792, 128), F32),
        jax.ShapeDtypeStruct((128, 1792), F32),
    )
    results = pl.pallas_call(
        kernel,
        name="expert_layer",
        out_shape=shapes,
        in_specs=[hbm] * 8,
        out_specs=(hbm,) * 5,
        scratch_shapes=[
            pltpu.VMEM((HALF, 128), BF16),
            pltpu.VMEM((HALF, 128), BF16),
            pltpu.VMEM((1792, 128), F32),
            pltpu.VMEM((1792, 128), F32),
            pltpu.VMEM((128, 1792), F32),
            sem((5,)),
            pltpu.VMEM((HALF, 128), BF16),
            pltpu.VMEM((HALF, 128), BF16),
            pltpu.VMEM((1, 128), jnp.int32),
            pltpu.VMEM((1, 128), F32),
            pltpu.VMEM((1, 32), jnp.int32),
            pltpu.VMEM((HALF, 256), BF16),
            pltpu.VMEM((2, HALF, 256), BF16),
            pltpu.VMEM((256, 256), BF16),
            pltpu.VMEM((16, 16, WIDE), BF16),
            pltpu.VMEM((2, CHUNKS, 2, 2, 2, 16, WIDE), BF16),
            pltpu.VMEM((2, WIDE, 256), BF16),
            pltpu.VMEM((128, 1792), BF16),
            pltpu.VMEM((CHUNKS, 64, 384), F32),
            pltpu.VMEM((CHUNKS, 64, 384), BF16),
            pltpu.VMEM((CHUNKS, 64, 384), BF16),
            pltpu.VMEM((CHUNKS, 64, 384), BF16),
            pltpu.VMEM((CHUNKS, 128, 384), BF16),
            pltpu.VMEM((CHUNKS, 2, 2, 2, 2, 16, WIDE), BF16),
            pltpu.VMEM((CHUNKS, 2, 2, 2, 16, WIDE), BF16),
            pltpu.VMEM((CHUNKS, 2, 2, 2, 16, WIDE), BF16),
            pltpu.VMEM((CHUNKS, 2, 1, 16, WIDE), BF16),
            pltpu.VMEM((CHUNKS, 2, 2, 16, WIDE), BF16),
            pltpu.VMEM((CHUNKS, 2, 16, WIDE), BF16),
            pltpu.VMEM((16, 16, WIDE), BF16),
            pltpu.VMEM((2, HALF, 256), BF16),
            pltpu.VMEM((HALF, 256), BF16),
            sem((5,)),
            sem((5,)),
            sem((2,)),
            sem((2,)),
            sem((CHUNKS + 1,)),
            sem((CHUNKS,)),
            sem((CHUNKS, 4)),
            sem((CHUNKS, 4)),
            sem((CHUNKS, 2)),
            sem((CHUNKS, 2)),
            sem((CHUNKS, 4)),
            sem((CHUNKS, 4)),
            sem((CHUNKS,)),
            sem((CHUNKS,)),
            sem((CHUNKS, 4)),
            sem((CHUNKS, 4)),
            sem((CHUNKS, 4)),
            sem((CHUNKS,)),
            sem,
            sem,
        ],
        compiler_params=pltpu.CompilerParams(
            collective_id=0, has_side_effects=True, vmem_limit_bytes=KERNEL_VMEM
        ),
    )(
        tokens.T,
        cotangent.T,
        route_ids.reshape(1, 128),
        gate_values.reshape(1, 128),
        slot_table.reshape(1, 32),
        w_gate,
        w_up,
        w_down,
    )
    mixed, back, grad_gate, grad_up, grad_down = pl.pallas_call(
        store,
        name="store",
        out_shape=shapes,
        in_specs=[hbm] * 5,
        out_specs=(hbm,) * 5,
        scratch_shapes=[pltpu.VMEM(shape.shape, shape.dtype) for shape in shapes] + [sem((2, 5))],
        compiler_params=pltpu.CompilerParams(vmem_limit_bytes=KERNEL_VMEM),
    )(*results)
    return mixed.T, back.T, grad_gate[None], grad_up[None], grad_down[None]


def solution(mesh):
    in_specs = (
        P(("attn", "shard"), "exp"),
        P(("attn", "shard"), None),
        P(("attn", "shard"), None),
        P(),
        P("attn", "shard", "exp"),
        P("attn", "shard", "exp"),
        P("attn", "exp", "shard"),
        P(("attn", "shard"), "exp"),
    )
    out_specs = (
        P(("attn", "shard"), "exp"),
        P(("attn", "shard"), "exp"),
        P("attn", "shard", "exp"),
        P("attn", "shard", "exp"),
        P("attn", "exp", "shard"),
    )
    return jax.shard_map(shards, mesh=mesh, in_specs=in_specs, out_specs=out_specs, check_vma=False)
```

```python
import jax
import jax.numpy as jnp
from jax import lax
from jax.experimental import pallas as pl
from jax.experimental.pallas import tpu as pltpu
from jax.sharding import PartitionSpec as P

CHUNKS = 8
LAGS = (0, 3, 4, 5, 7, 10, 11, 12)
WIDE = 896
HALF = 448
KERNEL_VMEM = 60 * 2**20
F32 = jnp.float32
BF16 = jnp.bfloat16


def base_offset(chunk):
    half = chunk // 2
    odd = jnp.where(chunk == 1, 4, 8 - half)
    return jnp.where(chunk % 2 == 0, half, odd)


def place():
    a, e, s = lax.axis_index("attn"), lax.axis_index("exp"), lax.axis_index("shard")
    return a % 4, a // 4 + 8 * s, e // 2, e % 2, s


def device(y, z, x, c):
    return {"attn": (z % 8) * 4 + y, "exp": 2 * x + c, "shard": z // 8}


def send(src, dst, send_sem, recv_sem, target):
    return pltpu.make_async_remote_copy(
        src_ref=src,
        dst_ref=dst,
        send_sem=send_sem,
        recv_sem=recv_sem,
        device_id=target,
        device_id_type=pl.DeviceIdType.MESH,
    )


def wait_for(ref, sem):
    pltpu.make_async_copy(ref, ref, sem).wait()


def last_last(a, b):
    return lax.dot_general(a, b, (((1,), (1,)), ((), ())), preferred_element_type=F32)


def first_first(a, b):
    return lax.dot_general(a, b, (((0,), (0,)), ((), ())), preferred_element_type=F32)


def dot(a, b):
    return jnp.dot(a, b, preferred_element_type=F32)


def kernel(
    tokens_far, cot_far, ids_far, gates_far, table_far, wg, wu, wd_far,
    mixed_far, back_far, gg_far, gu_far, gd_far, mixed, back, gg, gu, gd, g_s, tokens, cotangent, ids, gates, table, tok, ex, pp, sb, rows, wgu, wd, acc, es, em, er, lg, os, orr, cs, xr, rb, rr, tb, tr,
    i_r, w_r, tok_s, tok_r, d_s, d_r, ag_s, ag_r, sf_s, sf_r, e_s, e_r, o_s, o_r, x_s, x_r, b_s, b_r, t_s, t_r,
):
    y, z, x, c, s = place()
    other = 3 - x
    p_own = jnp.where(x // 2 == s, 0, 1)
    qi_own = jnp.where(p_own == 0, x, other) - 2 * s
    h_src = jnp.where(c == 0, x, other) // 2
    h_fin = x // 2
    x_fin = jnp.where(p_own == 0, x, other)
    has_self = (c == 0) & (p_own == 0)
    sibling = device(y, z, x, 1 - c)
    z_up, z_dn = device(y, (z + 4) % 16, x, c), device(y, (z + 12) % 16, x, c)

    def piece_of(xx):
        p = jnp.where(xx // 2 == s, 0, 1)
        return jnp.where(p == 0, xx, 3 - xx) - 2 * s, p

    loads = []
    for i, (far, near) in enumerate(
        ((tokens_far, tokens), (cot_far, cotangent), (ids_far, ids), (gates_far, gates), (table_far, table))
    ):
        loads.append(pltpu.make_async_copy(far, near, i_r.at[i]))
        loads[-1].start()

    barrier = pltpu.get_barrier_semaphore()

    def greet(target):
        pl.semaphore_signal(barrier, inc=1, device_id=target, device_id_type=pl.DeviceIdType.MESH)

    greet(sibling)
    greet(z_up)
    greet(z_dn)
    for r in (1, 2, 3):
        greet(device(y, z, (x + r) % 4, c))

    @pl.when(c == 0)
    def _():
        greet(device(y, z, x, 1))

    @pl.when(c == 1)
    def _():
        greet(device(y, z, other, 0))
        greet(device(y, z, other, 1))

    def greet_sources(i, carry):
        @pl.when(jnp.logical_not(has_self & (i == 0)))
        def _():
            greet(device((y + p_own + 2 * c) % 4, (z + i) % 16, x, p_own))

        return carry

    lax.fori_loop(0, 16, greet_sources, 0)
    x_back = jnp.where(c == 0, x, other)

    def greet_owners(i, carry):
        c_r = i % 2
        zz = 8 * h_fin + i // 2

        @pl.when(jnp.logical_not(has_self & (c_r == 0) & (zz == z)))
        def _():
            greet(device((y + 8 - c - 2 * c_r) % 4, zz, x_back, c_r))

        return carry

    lax.fori_loop(0, 16, greet_owners, 0)

    weights = [pltpu.make_async_copy(wd_far.at[0], wd, w_r.at[0])]
    for q in range(2):
        half = pl.ds(q * WIDE, WIDE)
        weights.append(pltpu.make_async_copy(wg.at[0, half], wgu.at[q, :, pl.ds(0, 128)], w_r.at[1 + q]))
        weights.append(pltpu.make_async_copy(wu.at[0, half], wgu.at[q, :, pl.ds(128, 128)], w_r.at[3 + q]))
    for load in weights:
        load.start()
    for load in loads:
        load.wait()

    tok[:, 0:128] = tokens[...]
    tok[:, 128:256] = (gates[...] * cotangent[...].astype(F32)).astype(BF16)

    pl.semaphore_wait(barrier, 7 + c + 32 - 2 * has_self.astype(jnp.int32))

    across = device(y, z, other, 1)

    @pl.when(c == 0)
    def _():
        send(tok, ex.at[0], tok_s.at[0], tok_r.at[0], across).start()

    @pl.when(c == 1)
    def _():
        send(tok, ex.at[1], tok_s.at[1], tok_r.at[1], device(y, z, x, 0)).start()
        send(tok, ex.at[1], tok_s.at[0], tok_r.at[1], across).start()

    row32 = lax.broadcasted_iota(jnp.int32, (32, 128), 0)
    named = (jnp.broadcast_to(ids[...], (32, 128)) == row32).astype(BF16)
    renamed = jnp.broadcast_to(table[...], (32, 32)) == lax.broadcasted_iota(jnp.int32, (32, 32), 0)
    member = dot(renamed.astype(BF16), named)
    earlier = lax.broadcasted_iota(jnp.int32, (128, 128), 0) < lax.broadcasted_iota(
        jnp.int32, (128, 128), 1
    )
    before = dot(member.astype(BF16), earlier.astype(BF16))
    rank_of = jnp.sum(member * before, axis=0, keepdims=True).astype(jnp.int32)
    slot_of = jnp.sum(member * row32.astype(F32), axis=0, keepdims=True).astype(jnp.int32)
    index = lax.broadcasted_iota(jnp.int32, (256, 128), 0)
    block, kind, rank = index // 16, (index // 8) % 2, index % 8
    offset = base_offset(block // 2)
    slot = ((z + 16 - offset) % 8) * 4 + (y + 8 - c - 2 * (block % 2)) % 4
    hit = (slot == slot_of) & (rank == rank_of)
    pp[:, 0:128] = (hit & (kind == 0)).astype(BF16)
    pp[:, 128:256] = (hit & (kind == 1)).astype(BF16)

    @pl.when(c == 0)
    def _():
        ex[0] = tok[...]

    @pl.when(c == 1)
    def _():
        wait_for(ex.at[0], tok_r.at[0])

    wait_for(ex.at[1], tok_r.at[1])
    sb[...] = last_last(pp[...], ex[...].reshape(WIDE, 256)).astype(BF16).reshape(16, 16, WIDE)

    def dispatch(i, carry):
        k, c_r = i // 2, i % 2
        zd = (z + 16 - base_offset(k)) % 16
        hi = jnp.where(zd // 8 == h_src, 0, 1)
        target = device((y + 8 - c - 2 * c_r) % 4, 8 * h_src + zd % 8, x, c_r)
        q_t = jnp.where(c == 0, x, other)
        there = rows.at[q_t - 2 * h_src, k, c_r, c, hi]
        mine = has_self & (i == 0)

        @pl.when(mine)
        def _():
            pltpu.make_async_copy(sb.at[i], there, d_r.at[k]).start()

        @pl.when(jnp.logical_not(mine))
        def _():
            send(sb.at[i], there, d_s.at[jnp.where(i == 0, CHUNKS, k)], d_r.at[k], target).start()

        return carry

    def give_out(k):
        lax.fori_loop(2 * k, 2 * k + 2, dispatch, 0)

    qi_up, p_up = piece_of((x + 1) % 4)
    qi_dn, p_dn = piece_of((x + 3) % 4)
    qi_far, p_far = piece_of((x + 2) % 4)
    first, second = pl.ds(0, 32), pl.ds(32, 32)

    def gather(k):
        own = rows.at[qi_own, k, c, p_own]
        wait_for(own, d_r.at[k])
        for r in (1, 2, 3):
            send(own, own, ag_s.at[k, r - 1], ag_r.at[k, r - 1], device(y, z, (x + r) % 4, c)).start()

    def forward(k):
        wait_for(rows.at[qi_dn, k, c, p_dn], ag_r.at[k, 0])
        wait_for(rows.at[qi_far, k, c, p_far], ag_r.at[k, 1])
        wait_for(rows.at[qi_up, k, c, p_up], ag_r.at[k, 2])
        for q in range(2):
            send(rows.at[q, k, c], rows.at[q, k, c], sf_s.at[k, q], sf_r.at[k, q], sibling).start()

    def project(k):
        for q in range(2):
            wait_for(rows.at[q, k, 1 - c], sf_r.at[k, q])
        both = jnp.zeros((128, 256), F32)
        down = jnp.zeros((128, 128), F32)
        for q in range(2):
            block = rows[q, k].reshape(128, WIDE)
            both = both + dot(block, wgu[q])
            down = down + last_last(block, wd[:, q * WIDE : (q + 1) * WIDE])
        part = jnp.concatenate(
            [both.reshape(8, 2, 8, 256)[:, 0], down.reshape(8, 2, 8, 128)[:, 1]], axis=-1
        )
        acc[k] = part.reshape(64, 384)
        pairs = part.reshape(4, 2, 8, 384)
        es[k] = jnp.concatenate([pairs[:, 1:], pairs[:, :1]], axis=1).reshape(64, 384).astype(BF16)
        send(es.at[k, first], em.at[k, first], e_s.at[k, 0], e_r.at[k, 0], z_up).start()
        send(es.at[k, second], em.at[k, second], e_s.at[k, 1], e_r.at[k, 1], z_dn).start()

    def hop(k):
        wait_for(em.at[k, first], e_r.at[k, 0])
        send(em.at[k, first], er.at[k, first], e_s.at[k, 2], e_r.at[k, 2], z_up).start()
        wait_for(em.at[k, second], e_r.at[k, 1])
        send(em.at[k, second], er.at[k, second], e_s.at[k, 3], e_r.at[k, 3], z_dn).start()

    def expand(k):
        wait_for(er.at[k, first], e_r.at[k, 2])
        wait_for(er.at[k, second], e_r.at[k, 3])
        total = acc[k] + er[k].astype(F32)
        gate, up, d_hid = total[:, :128], total[:, 128:256], total[:, 256:]
        sigma = jax.nn.sigmoid(gate)
        hidden = gate * sigma * up
        d_gate = d_hid * up * sigma * (1.0 + gate * (1.0 - sigma))
        d_up = d_hid * gate * sigma
        d_both = jnp.concatenate([d_gate, d_up], axis=1)
        nothing = jnp.zeros((8, 8, 128), F32)
        over = jnp.concatenate([d_both.reshape(8, 8, 256), nothing], axis=-1)
        under = jnp.concatenate([nothing, nothing, hidden.reshape(8, 8, 128)], axis=-1)
        lg[k] = jnp.stack([over, under], axis=1).reshape(128, 384).astype(BF16)
        hidden, d_both = hidden.astype(BF16), d_both.astype(BF16)
        for q in range(2):
            outs = dot(hidden, wd[:, q * WIDE : (q + 1) * WIDE]).reshape(8, 8, WIDE)
            ins = last_last(d_both, wgu[q]).reshape(8, 8, WIDE)
            shares = jnp.stack([outs, ins], axis=1).reshape(2, 2, 2, 16, WIDE).astype(BF16)
            os[k, 0, q] = shares[0]
            os[k, 1, q] = shares[1]
        send(os.at[k, 1 - c], orr.at[k], o_s.at[k], o_r.at[k], sibling).start()

    def scatter(k):
        wait_for(orr.at[k], o_r.at[k])
        for q in range(2):
            cs[k, q] = (os[k, c, q].astype(F32) + orr[k, q].astype(F32)).astype(BF16)
        for r, (qi, p) in enumerate(((qi_up, p_up), (qi_far, p_far), (qi_dn, p_dn))):
            there = device(y, z, (x + 1 + r) % 4, c)
            send(cs.at[k, qi, p], xr.at[k, r], x_s.at[k, r], x_r.at[k, r], there).start()

    def give_back(k):
        total = cs[k, qi_own, p_own].astype(F32)
        for r in range(3):
            wait_for(xr.at[k, r], x_r.at[k, r])
            total = total + xr[k, r].astype(F32)
        rb[k] = total.astype(BF16)
        there = rr.at[2 * k + c]
        for hi in range(2):
            zs = (z + base_offset(k) + 8 * hi) % 16
            target = device((y + p_own + 2 * c) % 4, zs, x_fin, p_own)
            go = send(rb.at[k, hi], there, b_s.at[k, hi], b_r.at[k], target)
            if hi == 0:
                mine = has_self & (k == 0)

                @pl.when(mine)
                def _():
                    pltpu.make_async_copy(rb.at[k, 0], there, b_r.at[k]).start()

                @pl.when(jnp.logical_not(mine))
                def _():
                    go.start()

            else:
                go.start()

    order = (give_out, gather, forward, project, hop, expand, scatter, give_back)
    stages = tuple(zip(order, LAGS))

    def weight_gradients(q):
        factors = lg[...].reshape(1024, 384).T

        def columns(n, carry):
            lanes = pl.ds(pl.multiple_of(n * 128, 128), 128)
            block = rows[q, :, :, :, :, :, lanes].reshape(1024, 128)
            grads = dot(factors, block)
            at = pl.ds(pl.multiple_of(q * WIDE + n * 128, 128), 128)
            gg[at, :] = grads[:128].T
            gu[at, :] = grads[128:256].T
            gd[:, at] = grads[256:]
            return carry

        lax.fori_loop(0, 7, columns, 0)

    def step(t, carry):
        for stage, lag in stages:

            @pl.when((t >= lag) & (t < lag + CHUNKS))
            def _():
                stage(t - lag)

        @pl.when(t == CHUNKS + LAGS[-1] - 2)
        def _():
            weight_gradients(0)

        return carry

    for load in weights:
        load.wait()
    lax.fori_loop(0, CHUNKS + LAGS[-1], step, 0)

    weight_gradients(1)
    stores = [
        pltpu.make_async_copy(near, far, g_s.at[i])
        for i, (near, far) in enumerate(
            ((mixed, mixed_far), (back, back_far), (gg, gg_far), (gu, gu_far), (gd, gd_far))
        )
    ]
    for copy in stores[2:]:
        copy.start()
    for k in range(CHUNKS - 1):
        wait_for(rr.at[pl.ds(2 * k, 2)], b_r.at[k])
    early = first_first(rr[0:14].reshape(224, WIDE), pp[0:224])
    wait_for(rr.at[pl.ds(14, 2)], b_r.at[CHUNKS - 1])
    spread = early + first_first(rr[14:16].reshape(32, WIDE), pp[224:256])
    tb[...] = spread.astype(BF16).reshape(2, HALF, 256)
    swap = send(tb.at[1 - c], tr, t_s, t_r, sibling)
    swap.start()

    wait_for(tok, tok_s.at[0])

    @pl.when(c == 1)
    def _():
        wait_for(tok, tok_s.at[1])

    wait_for(sb.at[1], d_s.at[0])
    for k in range(1, CHUNKS):
        wait_for(sb.at[pl.ds(2 * k, 2)], d_s.at[k])

    @pl.when(jnp.logical_not(has_self))
    def _():
        wait_for(sb.at[0], d_s.at[CHUNKS])
        wait_for(rb.at[0, 0], b_s.at[0, 0])

    def drain(k, carry):
        for r in range(3):
            wait_for(xr.at[k, r], x_s.at[k, r])
            wait_for(xr.at[k, r], ag_s.at[k, r])
        for q in range(2):
            wait_for(rows.at[q, k, c], sf_s.at[k, q])
        wait_for(es.at[k, first], e_s.at[k, 0])
        wait_for(es.at[k, second], e_s.at[k, 1])
        wait_for(em.at[k, first], e_s.at[k, 2])
        wait_for(em.at[k, second], e_s.at[k, 3])
        wait_for(orr.at[k], o_s.at[k])
        for i in range(2):
            if i == 0:

                @pl.when(k > 0)
                def _():
                    wait_for(rb.at[k, 0], b_s.at[k, 0])

            else:
                wait_for(rb.at[k, i], b_s.at[k, i])
        return carry

    lax.fori_loop(0, CHUNKS, drain, 0)
    swap.wait()
    mixed[...] = (gates[...] * (tb[c, :, 0:128] + tr[:, 0:128]).astype(F32)).astype(BF16)
    stores[0].start()
    back[...] = tb[c, :, 128:256] + tr[:, 128:256]
    stores[1].start()
    for copy in stores:
        copy.wait()


def store(*refs):
    far, out, near, sems = refs[0:5], refs[5:10], refs[10:15], refs[15]
    parts = []
    for i in (2, 3, 4, 0, 1):
        rows = far[i].shape[0]
        count = 4 if i > 1 else 1
        for n in range(count):
            parts.append((i, pl.ds(n * (rows // count), rows // count)))
    reads = [
        pltpu.make_async_copy(far[i].at[at], near[i].at[at], sems.at[0, n])
        for n, (i, at) in enumerate(parts)
    ]
    writes = [
        pltpu.make_async_copy(near[i].at[at], out[i].at[at], sems.at[1, n])
        for n, (i, at) in enumerate(parts)
    ]
    for read in reads:
        read.start()
    for read, write in zip(reads, writes):
        read.wait()
        write.start()
    for write in writes:
        write.wait()


def shards(tokens, route_ids, gate_values, slot_table, w_gate, w_up, w_down, cotangent):
    hbm = pl.BlockSpec(memory_space=pltpu.HBM)
    sem = pltpu.SemaphoreType.DMA
    shapes = (
        jax.ShapeDtypeStruct((HALF, 128), BF16),
        jax.ShapeDtypeStruct((HALF, 128), BF16),
        jax.ShapeDtypeStruct((1792, 128), F32),
        jax.ShapeDtypeStruct((1792, 128), F32),
        jax.ShapeDtypeStruct((128, 1792), F32),
    )
    results = pl.pallas_call(
        kernel,
        name="expert_layer",
        out_shape=shapes,
        in_specs=[hbm] * 8,
        out_specs=(hbm,) * 5,
        scratch_shapes=[
            pltpu.VMEM((HALF, 128), BF16),
            pltpu.VMEM((HALF, 128), BF16),
            pltpu.VMEM((1792, 128), F32),
            pltpu.VMEM((1792, 128), F32),
            pltpu.VMEM((128, 1792), F32),
            sem((5,)),
            pltpu.VMEM((HALF, 128), BF16),
            pltpu.VMEM((HALF, 128), BF16),
            pltpu.VMEM((1, 128), jnp.int32),
            pltpu.VMEM((1, 128), F32),
            pltpu.VMEM((1, 32), jnp.int32),
            pltpu.VMEM((HALF, 256), BF16),
            pltpu.VMEM((2, HALF, 256), BF16),
            pltpu.VMEM((256, 256), BF16),
            pltpu.VMEM((16, 16, WIDE), BF16),
            pltpu.VMEM((2, CHUNKS, 2, 2, 2, 16, WIDE), BF16),
            pltpu.VMEM((2, WIDE, 256), BF16),
            pltpu.VMEM((128, 1792), BF16),
            pltpu.VMEM((CHUNKS, 64, 384), F32),
            pltpu.VMEM((CHUNKS, 64, 384), BF16),
            pltpu.VMEM((CHUNKS, 64, 384), BF16),
            pltpu.VMEM((CHUNKS, 64, 384), BF16),
            pltpu.VMEM((CHUNKS, 128, 384), BF16),
            pltpu.VMEM((CHUNKS, 2, 2, 2, 2, 16, WIDE), BF16),
            pltpu.VMEM((CHUNKS, 2, 2, 2, 16, WIDE), BF16),
            pltpu.VMEM((CHUNKS, 2, 2, 2, 16, WIDE), BF16),
            pltpu.VMEM((CHUNKS, 3, 2, 16, WIDE), BF16),
            pltpu.VMEM((CHUNKS, 2, 16, WIDE), BF16),
            pltpu.VMEM((16, 16, WIDE), BF16),
            pltpu.VMEM((2, HALF, 256), BF16),
            pltpu.VMEM((HALF, 256), BF16),
            sem((5,)),
            sem((5,)),
            sem((2,)),
            sem((2,)),
            sem((CHUNKS + 1,)),
            sem((CHUNKS,)),
            sem((CHUNKS, 4)),
            sem((CHUNKS, 4)),
            sem((CHUNKS, 2)),
            sem((CHUNKS, 2)),
            sem((CHUNKS, 4)),
            sem((CHUNKS, 4)),
            sem((CHUNKS,)),
            sem((CHUNKS,)),
            sem((CHUNKS, 3)),
            sem((CHUNKS, 3)),
            sem((CHUNKS, 4)),
            sem((CHUNKS,)),
            sem,
            sem,
        ],
        compiler_params=pltpu.CompilerParams(
            collective_id=0, has_side_effects=True, vmem_limit_bytes=KERNEL_VMEM
        ),
    )(
        tokens.T,
        cotangent.T,
        route_ids.reshape(1, 128),
        gate_values.reshape(1, 128),
        slot_table.reshape(1, 32),
        w_gate,
        w_up,
        w_down,
    )
    mixed, back, grad_gate, grad_up, grad_down = pl.pallas_call(
        store,
        name="store",
        out_shape=shapes,
        in_specs=[hbm] * 5,
        out_specs=(hbm,) * 5,
        scratch_shapes=[pltpu.VMEM(shape.shape, shape.dtype) for shape in shapes] + [sem((2, 14))],
        compiler_params=pltpu.CompilerParams(vmem_limit_bytes=KERNEL_VMEM),
    )(*results)
    return mixed.T, back.T, grad_gate[None], grad_up[None], grad_down[None]


def solution(mesh):
    in_specs = (
        P(("attn", "shard"), "exp"),
        P(("attn", "shard"), None),
        P(("attn", "shard"), None),
        P(),
        P("attn", "shard", "exp"),
        P("attn", "shard", "exp"),
        P("attn", "exp", "shard"),
        P(("attn", "shard"), "exp"),
    )
    out_specs = (
        P(("attn", "shard"), "exp"),
        P(("attn", "shard"), "exp"),
        P("attn", "shard", "exp"),
        P("attn", "shard", "exp"),
        P("attn", "exp", "shard"),
    )
    return jax.shard_map(shards, mesh=mesh, in_specs=in_specs, out_specs=out_specs, check_vma=False)
```
